32 devices in a mesh: wide: 16 (over z, y, core), narrow: 2 (over x).
Axes of the slice: x: 2, y: 2, z: 4, core: 2. Of those that a mesh axis runs over, the one named last changes fastest.
Arguments:
- gradient: bfloat16 [40960, 8192], P(('wide', 'narrow')), may hold values from -81 to 81
- seating: int32 [32], replicated, may hold values from 0 to 31, each once
Outputs:
- rotated: bfloat16 [40960, 8192], P(('wide', 'narrow'))
The draws below stay inside these ranges and needn't reach their ends.
Inputs may be any that keep to these rules, and one draw needn't show every extreme that they name: `seating`: each of the 32 block numbers is the seat of exactly one block.
All inputs are finite; a program needn't handle non-finite values.
Results may differ from the reference program's by a relative error of at most 0.0075.
Values may be sent and summed in bfloat16 or wider, within the bound.
No kernel may reach another device: no remote copies, remote signals or barrier semaphores. Data moves between devices by JAX's collectives and lax.ppermute only.
A program may use at most 128 MiB of HBM per device.

```python
import math
import jax
import jax.numpy as jnp
from jax import lax

BW = 256
ROWS = 40960
ROUNDS = 8
STEPS = 2
BLOCKS = 32
COLS = 8192


def draw_gradient(key, part):
    keys = jax.random.split(key, 3)
    row_scale = jnp.exp(jax.random.uniform(keys[0], (ROWS, 1), jnp.float32, math.log(0.3), math.log(3.0)))
    col_scale = jnp.exp(jax.random.uniform(keys[1], (1, COLS), jnp.float32, math.log(0.3), math.log(3.0)))
    noise = jnp.clip(jax.random.normal(keys[2], (ROWS, COLS), jnp.float32), -5.0, 5.0)
    values = noise * row_scale * col_scale
    return values.astype(jnp.bfloat16)


def setup_inputs(seed: int = 0) -> dict:
    key_list = jax.random.split(jax.random.key(seed), 3)
    return {
        "gradient": draw_gradient(jax.random.fold_in(key_list[2], 71), 0),
        "seating": jax.random.permutation(key_list[1], BLOCKS).astype(jnp.int32),
    }


def advance(seat_of, total_slots):
    pair_count = total_slots // 2
    cycle_pos = jnp.where(seat_of % 2 == 0, seat_of // 2 - 1, total_slots - 2 - (seat_of - 1) // 2)
    next_pos = (cycle_pos + 1) % (total_slots - 1)
    new_slot = jnp.where(next_pos < pair_count - 1, 2 * (next_pos + 1), 2 * (total_slots - 2 - next_pos) + 1)
    return jnp.where(seat_of == 0, 0, new_slot).astype(jnp.int32)

def occupants(seat_of, total_slots):
    block_ids = jnp.arange(total_slots, dtype=jnp.int32)
    matches = seat_of[None, :] == block_ids[:, None]
    return lax.optimization_barrier(jnp.sum(jnp.where(matches, block_ids[None, :], 0), axis=1)).astype(jnp.int32)

def rotate_columns(matrix, cosine, sine_part):
    width = cosine.shape[0]
    left_cols = matrix[:, :width]
    right_cols = matrix[:, width:]
    return jnp.concatenate([left_cols * cosine - right_cols * sine_part, left_cols * sine_part + right_cols * cosine], axis=1)

def roll_second(matrix, offset, which_axis):
    head_part, tail_part = jnp.split(matrix, 2, axis=which_axis)
    return jnp.concatenate([head_part, jnp.roll(tail_part, offset, axis=which_axis)], axis=which_axis)

def one_round(round_index, carried):
    gram_mat, rotation = carried
    width = gram_mat.shape[0] // 2
    left_diag = jnp.diagonal(gram_mat[:width, :width])
    right_diag = jnp.diagonal(gram_mat[width:, width:])
    off_diag = jnp.diagonal(gram_mat[:width, width:])
    spread = right_diag - left_diag
    damping = (left_diag + right_diag) / 16.0 + 1e-06
    radius = jnp.sqrt(spread * spread + 4.0 * off_diag * off_diag + damping * damping)
    tangent = 2.0 * off_diag / (spread + radius)
    cosine = 1.0 / jnp.sqrt(1.0 + tangent * tangent)
    sine_part = tangent * cosine
    gram_mat = rotate_columns(gram_mat, cosine, sine_part)
    gram_mat = rotate_columns(gram_mat.T, cosine, sine_part).T
    rotation = rotate_columns(rotation, cosine, sine_part)
    gram_mat = roll_second(roll_second(gram_mat, -1, 0), -1, 1)
    rotation = roll_second(rotation, -1, 1)
    return (gram_mat, rotation)

def rotations(gram_mat):
    initial = (gram_mat, jnp.eye(gram_mat.shape[0], dtype=jnp.float32))
    gram_mat, rotation = lax.fori_loop(0, ROUNDS, one_round, initial)
    return roll_second(rotation, ROUNDS, 1)

def update_pair(pair_data):
    gram_mat = jnp.dot(pair_data.T, pair_data, preferred_element_type=jnp.float32)
    rotation = rotations(gram_mat).astype(jnp.bfloat16)
    return jnp.dot(pair_data, rotation, preferred_element_type=jnp.float32).astype(jnp.bfloat16)

def reference(gradient, seating):
    blocks_all = gradient.reshape(ROWS, BLOCKS, BW)
    seat_of = seating.astype(jnp.int32)
    for section_index in range(STEPS):
        if section_index > 0:
            seat_of = advance(seat_of, BLOCKS)
        holders = occupants(seat_of, BLOCKS)
        seated = jnp.take(blocks_all, holders, axis=1)
        pair_data = seated.reshape(ROWS, BLOCKS // 2, 2 * BW).transpose(1, 0, 2)
        new_pairs = lax.map(update_pair, pair_data)
        seated = new_pairs.transpose(1, 0, 2).reshape(ROWS, BLOCKS, BW)
        blocks_all = jnp.take(seated, seat_of, axis=1)
    return blocks_all.reshape(ROWS, COLS)
```

```python
import functools

import jax
import jax.numpy as jnp
from jax import lax
from jax.experimental import pallas as pl
from jax.experimental.pallas import tpu as pltpu
from jax.sharding import PartitionSpec as P

ROUNDS = 8
LANES = 128
VMEM_LIMIT = 56 * 1024 * 1024


def advance(seat_of, total_slots):
    pair_count = total_slots // 2
    cycle_pos = jnp.where(seat_of % 2 == 0, seat_of // 2 - 1, total_slots - 2 - (seat_of - 1) // 2)
    next_pos = (cycle_pos + 1) % (total_slots - 1)
    new_slot = jnp.where(
        next_pos < pair_count - 1, 2 * (next_pos + 1), 2 * (total_slots - 2 - next_pos) + 1
    )
    return jnp.where(seat_of == 0, 0, new_slot)


def cyclic_masks(width):
    row = lax.broadcasted_iota(jnp.int32, (width, width), 0)
    col = lax.broadcasted_iota(jnp.int32, (width, width), 1)
    gap = col - row
    above = jnp.where(gap < 0, gap + width, gap) < ROUNDS
    below = jnp.where(gap > 0, width - gap, -gap) < ROUNDS
    return above, below


def fold(block, mask):
    width = block.shape[0]
    kept = jnp.where(mask, block, 0.0)
    return jnp.sum(kept.reshape(width // ROUNDS, ROUNDS, width), axis=0)


def unfolded(folded, mask):
    width = folded.shape[1]
    tiled = jnp.broadcast_to(folded[None], (width // ROUNDS, ROUNDS, width))
    return jnp.where(mask, tiled.reshape(width, width), 0.0)


def gram_diagonals(left, right):
    width = left.shape[1]
    above, below = cyclic_masks(width)
    over_rows = (((0,), (0,)), ((), ()))
    dot = functools.partial(
        lax.dot_general, dimension_numbers=over_rows, preferred_element_type=jnp.float32
    )
    cross = dot(left, right)
    return jnp.concatenate(
        [fold(dot(left, left), above), fold(cross, below), fold(cross, above), fold(dot(right, right), above)],
        axis=0,
    )


def pick(planes, index):
    out = planes[0]
    for place in range(1, len(planes)):
        out = jnp.where(index == place, planes[place], out)
    return out


def roll_lanes(plane, shift):
    width = plane.shape[1]
    shift = shift % width
    return plane if shift == 0 else pltpu.roll(plane, shift, 1)


def blend(c, u, s, v, sign):
    if u is None and v is None:
        return None
    if u is None:
        return s * v if sign > 0 else -(s * v)
    if v is None:
        return c * u
    return c * u + s * v if sign > 0 else c * u - s * v


def rotation_diagonals(load):
    lane = lax.broadcasted_iota(jnp.int32, load(0, 0).shape, 1)
    residue = lane % ROUNDS
    quarters = []
    for q in range(4):
        rows = [load(q, s) for s in range(ROUNDS)]
        if q == 1:
            planes = [pick(rows, (residue + d) % ROUNDS) for d in range(ROUNDS)]
            planes = [roll_lanes(plane, d) for d, plane in enumerate(planes)]
        else:
            planes = [pick(rows, (residue - d) % ROUNDS) for d in range(ROUNDS)]
        quarters.append(planes)
    ll, lr, rl, rr = quarters
    ones = jnp.ones_like(ll[0])
    tl, bl = [ones] + [None] * 7, [None] * 8
    tr, br = [None] * 8, [ones] + [None] * 7
    for r in range(ROUNDS):
        a, c, off = ll[0], rr[0], rl[0]
        spread = c - a
        damping = (a + c) / 16.0 + 1e-06
        rest = 4.0 * off * off + damping * damping
        radius = jnp.sqrt(spread * spread + rest)
        falling = spread < 0.0
        reach = radius + jnp.abs(spread)
        tangent = 2.0 * off * jnp.where(falling, reach, 1.0) / jnp.where(falling, rest, reach)
        cs = 1.0 / jnp.sqrt(1.0 + tangent * tangent)
        sn = tangent * cs
        for rows_l, rows_r in ((tl, tr), (bl, br)):
            for o in range(ROUNDS):
                u, v = rows_l[o], rows_r[o]
                rows_l[o] = blend(cs, u, sn, v, -1)
                rows_r[o] = blend(cs, v, sn, u, 1)
        if r + 1 == ROUNDS:
            break
        needed = ROUNDS - r
        new = [[], [], [], []]
        for d in range(needed):
            cl, sl = roll_lanes(cs, d), roll_lanes(sn, d)
            ll1 = cl * ll[d] - sl * lr[d]
            lr1 = sl * ll[d] + cl * lr[d]
            rl1 = cl * rl[d] - sl * rr[d]
            rr1 = sl * rl[d] + cl * rr[d]
            new[0].append(cs * ll1 - sn * rl1)
            new[1].append(cs * lr1 - sn * rr1)
            new[2].append(sn * ll1 + cs * rl1)
            new[3].append(sn * lr1 + cs * rr1)
        ll = new[0][: needed - 1]
        rl = [roll_lanes(plane, -1) for plane in new[2][1:needed]]
        lr = [rl[0]] + new[1][: needed - 2]
        rr = [roll_lanes(plane, -1) for plane in new[3][: needed - 1]]
        for rows_r in (tr, br):
            rows_r[:] = [None] + [
                None if plane is None else roll_lanes(plane, -1) for plane in rows_r[:-1]
            ]
    folded = []
    for rows in (tl, bl):
        folded.append([pick(rows, (s - residue) % ROUNDS) for s in range(ROUNDS)])
    for rows in (tr, br):
        turned = [roll_lanes(plane, ROUNDS - 1) for plane in rows[::-1]]
        folded.append([pick(turned, (residue - s) % ROUNDS) for s in range(ROUNDS)])
    return folded


def find_holders(seat_ref, holder_ref):
    for block in range(holder_ref.shape[0]):
        holder_ref[seat_ref[block]] = block


def block_copies(pair, holder_ref, outer_ref, pair_buffer, sems, inward):
    width = pair_buffer.shape[2] // 2
    copies = []
    for half in range(2):
        column = pl.multiple_of(holder_ref[2 * pair + half] * width, width)
        outer = outer_ref.at[:, pl.ds(column, width)]
        inner = pair_buffer.at[pair, :, pl.ds(half * width, width)]
        source, target = (outer, inner) if inward else (inner, outer)
        copies.append(pltpu.make_async_copy(source, target, sems.at[2 * pair + half]))
    return copies


def start_all(pairs, make):
    def body(pair, carry):
        for copy in make(pair):
            copy.start()
        return carry

    lax.fori_loop(0, pairs, body, 0)


def wait_all(pairs, make):
    def body(pair, carry):
        for copy in make(pair):
            copy.wait()
        return carry

    lax.fori_loop(0, pairs, body, 0)


def put_pair(ref, pair, value):
    rows = pl.ds(pl.multiple_of(pair * 4 * ROUNDS, 4 * ROUNDS), 4 * ROUNDS)
    for part in range(ref.shape[0]):
        ref[part, rows, :] = value[:, part * LANES : (part + 1) * LANES]


def get_quarter(ref, pair, q):
    rows = pl.ds(pl.multiple_of((pair * 4 + q) * ROUNDS, ROUNDS), ROUNDS)
    return jnp.concatenate([ref[part, rows, :] for part in range(ref.shape[0])], axis=1)


def gram_kernel(seat_ref, x_ref, diag_ref, held, holder_ref, in_sems):
    pairs, _, both = held.shape
    width = both // 2
    find_holders(seat_ref, holder_ref)
    arrive = lambda pair: block_copies(pair, holder_ref, x_ref, held, in_sems, True)
    start_all(pairs, arrive)

    def body(pair, carry):
        for copy in arrive(pair):
            copy.wait()
        put_pair(diag_ref, pair, gram_diagonals(held[pair, :, :width], held[pair, :, width:]))
        return carry

    lax.fori_loop(0, pairs, body, 0)


def store_rotation(diag_ref, fold_ref):
    parts, rows, _ = diag_ref.shape
    pairs = rows // (4 * ROUNDS)
    plane = lambda q, s: pl.ds(q * ROUNDS + s, pairs, stride=4 * ROUNDS)
    load = lambda q, s: jnp.concatenate(
        [diag_ref[part, plane(q, s), :] for part in range(parts)], axis=1
    )
    folded = rotation_diagonals(load)
    for q in range(4):
        for s in range(ROUNDS):
            for part in range(parts):
                columns = slice(part * LANES, (part + 1) * LANES)
                fold_ref[part, plane(q, s), :] = folded[q][s][:, columns]


def rotate_pair(pair, held, fold_ref, dense_ref):
    width = held.shape[2] // 2
    above, below = cyclic_masks(width)
    quarter = lambda q: get_quarter(fold_ref, pair, q)
    dense_ref[:width, :width] = unfolded(quarter(0), below).astype(jnp.bfloat16)
    dense_ref[width:, :width] = unfolded(quarter(1), below).astype(jnp.bfloat16)
    dense_ref[:width, width:] = unfolded(quarter(2), above).astype(jnp.bfloat16)
    dense_ref[width:, width:] = unfolded(quarter(3), above).astype(jnp.bfloat16)
    turned = jnp.dot(held[pair], dense_ref[...], preferred_element_type=jnp.float32)
    held[pair] = turned.astype(jnp.bfloat16)


def apply_kernel(with_gram, seat_ref, diag_ref, x_ref, *refs):
    if with_gram:
        out_ref, next_ref, held, fold_ref, dense_ref, holder_ref, in_sems, out_sems = refs
    else:
        out_ref, held, fold_ref, dense_ref, holder_ref, in_sems, out_sems = refs
    pairs, _, both = held.shape
    width = both // 2
    find_holders(seat_ref, holder_ref)
    arrive = lambda pair: block_copies(pair, holder_ref, x_ref, held, in_sems, True)
    leave = lambda pair: block_copies(pair, holder_ref, out_ref, held, out_sems, False)
    start_all(pairs, arrive)
    store_rotation(diag_ref, fold_ref)

    def next_gram(pair):
        left_seat = jnp.where(pair == 0, 0, jnp.where(pair == 1, 1, 2 * pair - 2))
        right_seat = jnp.where(pair == pairs - 1, 2 * pairs - 2, 2 * pair + 3)

        def block(seat):
            column = pl.multiple_of((seat % 2) * width, width)
            return held[seat // 2, :, pl.ds(column, width)]

        put_pair(next_ref, pair, gram_diagonals(block(left_seat), block(right_seat)))

    def body(pair, carry):
        for copy in arrive(pair):
            copy.wait()
        rotate_pair(pair, held, fold_ref, dense_ref)
        for copy in leave(pair):
            copy.start()
        if with_gram:
            pl.when(pair > 0)(lambda: next_gram(pair - 1))
        return carry

    lax.fori_loop(0, pairs, body, 0)
    if with_gram:
        next_gram(pairs - 1)
    wait_all(pairs, leave)


def per_device(gradient, seating):
    rows, columns = gradient.shape
    pairs = lax.axis_size("wide")
    width = columns // (2 * pairs)
    everywhere = ("wide", "narrow")
    following = advance(seating, 2 * pairs)

    smem = pl.BlockSpec(memory_space=pltpu.SMEM)
    vmem = pl.BlockSpec(memory_space=pltpu.VMEM)
    hbm = pl.BlockSpec(memory_space=pl.ANY)
    params = pltpu.CompilerParams(vmem_limit_bytes=VMEM_LIMIT)
    held = pltpu.VMEM((pairs, rows, 2 * width), jnp.bfloat16)
    holders = pltpu.SMEM((2 * pairs,), jnp.int32)
    sems = pltpu.SemaphoreType.DMA((2 * pairs,))
    fold = pltpu.VMEM((width // LANES, pairs * 4 * ROUNDS, LANES), jnp.float32)
    dense = pltpu.VMEM((2 * width, 2 * width), jnp.bfloat16)
    diag_shape = jax.ShapeDtypeStruct((width // LANES, pairs * 4 * ROUNDS, LANES), jnp.float32)
    x_shape = jax.ShapeDtypeStruct((rows, columns), jnp.bfloat16)
    gram_flops = 2 * rows * 3 * width * width * pairs
    turn_flops = 2 * rows * 4 * width * width * pairs
    x_bytes = 2 * rows * columns
    cost = lambda flops, moved: pl.CostEstimate(flops=flops, bytes_accessed=moved, transcendentals=0)

    diagonals = pl.pallas_call(
        gram_kernel,
        out_shape=diag_shape,
        in_specs=[smem, hbm],
        out_specs=vmem,
        scratch_shapes=[held, holders, sems],
        compiler_params=params,
        cost_estimate=cost(gram_flops, x_bytes),
        name="gram_of_step_0",
    )(seating, gradient)
    diagonals = lax.psum(diagonals, everywhere)

    turned, diagonals = pl.pallas_call(
        functools.partial(apply_kernel, True),
        out_shape=(x_shape, diag_shape),
        in_specs=[smem, vmem, hbm],
        out_specs=(hbm, vmem),
        scratch_shapes=[held, fold, dense, holders, sems, sems],
        compiler_params=params,
        cost_estimate=cost(gram_flops + turn_flops, 2 * x_bytes),
        name="rotate_step_0",
    )(seating, diagonals, gradient)
    diagonals = lax.psum(diagonals, everywhere)

    return pl.pallas_call(
        functools.partial(apply_kernel, False),
        out_shape=x_shape,
        in_specs=[smem, vmem, hbm],
        out_specs=hbm,
        scratch_shapes=[held, fold, dense, holders, sems, sems],
        compiler_params=params,
        cost_estimate=cost(turn_flops, 2 * x_bytes),
        name="rotate_step_1",
    )(following, diagonals, turned)


def solution(mesh):
    in_specs = (P(("wide", "narrow"), None), P())
    out_specs = P(("wide", "narrow"), None)
    return jax.shard_map(
        per_device, mesh=mesh, in_specs=in_specs, out_specs=out_specs, check_vma=False
    )
```

```python
import functools

import jax
import jax.numpy as jnp
from jax import lax
from jax.experimental import pallas as pl
from jax.experimental.pallas import tpu as pltpu
from jax.sharding import PartitionSpec as P

ROUNDS = 8
LANES = 128
VMEM_LIMIT = 56 * 1024 * 1024


def advance(seat_of, total_slots):
    pair_count = total_slots // 2
    cycle_pos = jnp.where(seat_of % 2 == 0, seat_of // 2 - 1, total_slots - 2 - (seat_of - 1) // 2)
    next_pos = (cycle_pos + 1) % (total_slots - 1)
    new_slot = jnp.where(
        next_pos < pair_count - 1, 2 * (next_pos + 1), 2 * (total_slots - 2 - next_pos) + 1
    )
    return jnp.where(seat_of == 0, 0, new_slot)


def cyclic_masks(width):
    row = lax.broadcasted_iota(jnp.int32, (width, width), 0)
    col = lax.broadcasted_iota(jnp.int32, (width, width), 1)
    gap = col - row
    above = jnp.where(gap < 0, gap + width, gap) < ROUNDS
    below = jnp.where(gap > 0, width - gap, -gap) < ROUNDS
    return above, below


def fold(block, mask):
    width = block.shape[0]
    kept = jnp.where(mask, block, 0.0)
    return jnp.sum(kept.reshape(width // ROUNDS, ROUNDS, width), axis=0)


def unfolded(folded, mask):
    width = folded.shape[1]
    tiled = jnp.broadcast_to(folded[None], (width // ROUNDS, ROUNDS, width))
    return jnp.where(mask, tiled.reshape(width, width), 0.0)


def gram_diagonals(left, right):
    width = left.shape[1]
    above, below = cyclic_masks(width)
    over_rows = (((0,), (0,)), ((), ()))
    dot = functools.partial(
        lax.dot_general, dimension_numbers=over_rows, preferred_element_type=jnp.float32
    )
    cross = dot(left, right)
    return jnp.concatenate(
        [fold(dot(left, left), above), fold(cross, below), fold(cross, above), fold(dot(right, right), above)],
        axis=0,
    )


def pick(planes, index):
    out = planes[0]
    for place in range(1, len(planes)):
        out = jnp.where(index == place, planes[place], out)
    return out


def roll_lanes(plane, shift):
    width = plane.shape[1]
    shift = shift % width
    return plane if shift == 0 else pltpu.roll(plane, shift, 1)


def blend(c, u, s, v, sign):
    if u is None and v is None:
        return None
    if u is None:
        return s * v if sign > 0 else -(s * v)
    if v is None:
        return c * u
    return c * u + s * v if sign > 0 else c * u - s * v


def rotation_diagonals(load):
    lane = lax.broadcasted_iota(jnp.int32, load(0, 0).shape, 1)
    residue = lane % ROUNDS
    quarters = []
    for q in range(4):
        rows = [load(q, s) for s in range(ROUNDS)]
        if q == 1:
            planes = [pick(rows, (residue + d) % ROUNDS) for d in range(ROUNDS)]
            planes = [roll_lanes(plane, d) for d, plane in enumerate(planes)]
        else:
            planes = [pick(rows, (residue - d) % ROUNDS) for d in range(ROUNDS)]
        quarters.append(planes)
    ll, lr, rl, rr = quarters
    ones = jnp.ones_like(ll[0])
    tl, bl = [ones] + [None] * 7, [None] * 8
    tr, br = [None] * 8, [ones] + [None] * 7
    for r in range(ROUNDS):
        a, c, off = ll[0], rr[0], rl[0]
        spread = c - a
        damping = (a + c) / 16.0 + 1e-06
        rest = 4.0 * off * off + damping * damping
        radius = jnp.sqrt(spread * spread + rest)
        falling = spread < 0.0
        reach = radius + jnp.abs(spread)
        tangent = 2.0 * off * jnp.where(falling, reach, 1.0) / jnp.where(falling, rest, reach)
        cs = 1.0 / jnp.sqrt(1.0 + tangent * tangent)
        sn = tangent * cs
        for rows_l, rows_r in ((tl, tr), (bl, br)):
            for o in range(ROUNDS):
                u, v = rows_l[o], rows_r[o]
                rows_l[o] = blend(cs, u, sn, v, -1)
                rows_r[o] = blend(cs, v, sn, u, 1)
        if r + 1 == ROUNDS:
            break
        needed = ROUNDS - r
        new = [[], [], [], []]
        for d in range(needed):
            cl, sl = roll_lanes(cs, d), roll_lanes(sn, d)
            ll1 = cl * ll[d] - sl * lr[d]
            lr1 = sl * ll[d] + cl * lr[d]
            rl1 = cl * rl[d] - sl * rr[d]
            rr1 = sl * rl[d] + cl * rr[d]
            new[0].append(cs * ll1 - sn * rl1)
            new[1].append(cs * lr1 - sn * rr1)
            new[2].append(sn * ll1 + cs * rl1)
            new[3].append(sn * lr1 + cs * rr1)
        ll = new[0][: needed - 1]
        rl = [roll_lanes(plane, -1) for plane in new[2][1:needed]]
        lr = [rl[0]] + new[1][: needed - 2]
        rr = [roll_lanes(plane, -1) for plane in new[3][: needed - 1]]
        for rows_r in (tr, br):
            rows_r[:] = [None] + [
                None if plane is None else roll_lanes(plane, -1) for plane in rows_r[:-1]
            ]
    folded = []
    for rows in (tl, bl):
        folded.append([pick(rows, (s - residue) % ROUNDS) for s in range(ROUNDS)])
    for rows in (tr, br):
        turned = [roll_lanes(plane, ROUNDS - 1) for plane in rows[::-1]]
        folded.append([pick(turned, (residue - s) % ROUNDS) for s in range(ROUNDS)])
    return folded


def find_holders(seat_ref, holder_ref):
    for block in range(holder_ref.shape[0]):
        holder_ref[seat_ref[block]] = block


def block_copies(pair, holder_ref, outer_ref, pair_buffer, sems, inward):
    width = pair_buffer.shape[2] // 2
    copies = []
    for half in range(2):
        column = pl.multiple_of(holder_ref[2 * pair + half] * width, width)
        outer = outer_ref.at[:, pl.ds(column, width)]
        inner = pair_buffer.at[pair, :, pl.ds(half * width, width)]
        source, target = (outer, inner) if inward else (inner, outer)
        copies.append(pltpu.make_async_copy(source, target, sems.at[2 * pair + half]))
    return copies


def start_all(pairs, make):
    def body(pair, carry):
        for copy in make(pair):
            copy.start()
        return carry

    lax.fori_loop(0, pairs, body, 0)


def wait_all(pairs, make):
    def body(pair, carry):
        for copy in make(pair):
            copy.wait()
        return carry

    lax.fori_loop(0, pairs, body, 0)


def put_pair(ref, pair, value):
    rows = pl.ds(pl.multiple_of(pair * 4 * ROUNDS, 4 * ROUNDS), 4 * ROUNDS)
    for part in range(ref.shape[0]):
        ref[part, rows, :] = value[:, part * LANES : (part + 1) * LANES]


def get_quarter(ref, pair, q):
    rows = pl.ds(pl.multiple_of((pair * 4 + q) * ROUNDS, ROUNDS), ROUNDS)
    return jnp.concatenate([ref[part, rows, :] for part in range(ref.shape[0])], axis=1)


def gram_kernel(seat_ref, x_ref, diag_ref, held, holder_ref, in_sems):
    pairs, _, both = held.shape
    width = both // 2
    find_holders(seat_ref, holder_ref)
    arrive = lambda pair: block_copies(pair, holder_ref, x_ref, held, in_sems, True)
    start_all(pairs, arrive)

    def body(pair, carry):
        for copy in arrive(pair):
            copy.wait()
        put_pair(diag_ref, pair, gram_diagonals(held[pair, :, :width], held[pair, :, width:]))
        return carry

    lax.fori_loop(0, pairs, body, 0, unroll=2)


def store_rotation(diag_ref, fold_ref):
    parts, rows, _ = diag_ref.shape
    pairs = rows // (4 * ROUNDS)
    plane = lambda q, s: pl.ds(q * ROUNDS + s, pairs, stride=4 * ROUNDS)
    load = lambda q, s: jnp.concatenate(
        [diag_ref[part, plane(q, s), :] for part in range(parts)], axis=1
    )
    folded = rotation_diagonals(load)
    for q in range(4):
        for s in range(ROUNDS):
            for part in range(parts):
                columns = slice(part * LANES, (part + 1) * LANES)
                fold_ref[part, plane(q, s), :] = folded[q][s][:, columns]


def rotate_pair(pair, held, fold_ref, dense_ref):
    width = held.shape[2] // 2
    above, below = cyclic_masks(width)
    quarter = lambda q: get_quarter(fold_ref, pair, q)
    dense_ref[:width, :width] = unfolded(quarter(0), below).astype(jnp.bfloat16)
    dense_ref[width:, :width] = unfolded(quarter(1), below).astype(jnp.bfloat16)
    dense_ref[:width, width:] = unfolded(quarter(2), above).astype(jnp.bfloat16)
    dense_ref[width:, width:] = unfolded(quarter(3), above).astype(jnp.bfloat16)
    return jnp.dot(held[pair], dense_ref[...], preferred_element_type=jnp.float32)


def apply_kernel(with_gram, seat_ref, diag_ref, x_ref, *refs):
    if with_gram:
        out_ref, next_ref, held, fold_ref, dense_ref, holder_ref, in_sems, out_sems = refs
    else:
        out_ref, held, fold_ref, dense_ref, holder_ref, in_sems, out_sems = refs
    pairs, _, both = held.shape
    width = both // 2
    find_holders(seat_ref, holder_ref)
    arrive = lambda pair: block_copies(pair, holder_ref, x_ref, held, in_sems, True)
    leave = lambda pair: block_copies(pair, holder_ref, out_ref, held, out_sems, False)
    start_all(pairs, arrive)
    store_rotation(diag_ref, fold_ref)

    def next_gram(pair):
        left_seat = jnp.where(pair == 0, 0, jnp.where(pair == 1, 1, 2 * pair - 2))
        right_seat = jnp.where(pair == pairs - 1, 2 * pairs - 2, 2 * pair + 3)

        def block(seat):
            column = pl.multiple_of((seat % 2) * width, width)
            return held[seat // 2, :, pl.ds(column, width)]

        put_pair(next_ref, pair, gram_diagonals(block(left_seat), block(right_seat)))

    def body(step, carry):
        duo = (2 * step, 2 * step + 1)
        for pair in duo:
            for copy in arrive(pair):
                copy.wait()
        turned = [
            rotate_pair(pair, held, fold_ref, dense_ref.at[slot]) for slot, pair in enumerate(duo)
        ]
        for pair, value in zip(duo, turned):
            held[pair] = value.astype(jnp.bfloat16)
        for pair in duo:
            for copy in leave(pair):
                copy.start()
        if with_gram:
            pl.when(step > 0)(lambda: next_gram(duo[0] - 1))
            next_gram(duo[0])
        return carry

    lax.fori_loop(0, pairs // 2, body, 0)
    if with_gram:
        next_gram(pairs - 1)
    wait_all(pairs, leave)


def exchange_stages(axes):
    wide, narrow = (lax.axis_size(axis) for axis in axes)
    lower = [1 << b for b in range(narrow.bit_length() - 1)]
    upper = [narrow << b for b in range(wide.bit_length() - 1)]
    rest = lower + upper[1:]
    return [upper[:1]] + [rest[at : at + 2] for at in range(0, len(rest), 2)]


def sum_over_devices(values, axes):
    count = lax.axis_size(axes)
    index = lax.axis_index(axes)
    held = values.reshape(values.shape[0] * values.shape[1], LANES)

    def spread(choice, bits):
        return sum(bit for place, bit in enumerate(bits) if choice >> place & 1)

    def swap(x, flip):
        return lax.ppermute(x, axes, [(i, i ^ flip) for i in range(count)])

    def place_of(bits):
        return sum(((index & bit) != 0).astype(jnp.int32) << place for place, bit in enumerate(bits))

    stages = exchange_stages(axes)
    for bits in stages:
        group = 1 << len(bits)
        size = held.shape[0] // group
        me = place_of(bits)
        part = lambda place: lax.dynamic_slice_in_dim(held, place * size, size, 0)
        arrived = [swap(part(me ^ other), spread(other, bits)) for other in range(1, group)]
        held = functools.reduce(jnp.add, arrived, part(me))
    for bits in stages[::-1]:
        group = 1 << len(bits)
        me = place_of(bits)
        parts = [held] + [swap(held, spread(other, bits)) for other in range(1, group)]
        for place, _ in enumerate(bits):
            odd = (me >> place & 1) != 0
            step = 1 << place
            parts = [jnp.where(odd, parts[at ^ step], parts[at]) for at in range(group)]
        held = jnp.concatenate(parts, axis=0)
    return held.reshape(values.shape)


def per_device(gradient, seating):
    rows, columns = gradient.shape
    pairs = lax.axis_size("wide")
    width = columns // (2 * pairs)
    everywhere = ("wide", "narrow")
    following = advance(seating, 2 * pairs)

    smem = pl.BlockSpec(memory_space=pltpu.SMEM)
    vmem = pl.BlockSpec(memory_space=pltpu.VMEM)
    hbm = pl.BlockSpec(memory_space=pl.ANY)
    params = pltpu.CompilerParams(vmem_limit_bytes=VMEM_LIMIT)
    held = pltpu.VMEM((pairs, rows, 2 * width), jnp.bfloat16)
    holders = pltpu.SMEM((2 * pairs,), jnp.int32)
    sems = pltpu.SemaphoreType.DMA((2 * pairs,))
    fold = pltpu.VMEM((width // LANES, pairs * 4 * ROUNDS, LANES), jnp.float32)
    dense = pltpu.VMEM((2, 2 * width, 2 * width), jnp.bfloat16)
    diag_shape = jax.ShapeDtypeStruct((width // LANES, pairs * 4 * ROUNDS, LANES), jnp.float32)
    x_shape = jax.ShapeDtypeStruct((rows, columns), jnp.bfloat16)
    gram_flops = 2 * rows * 3 * width * width * pairs
    turn_flops = 2 * rows * 4 * width * width * pairs
    x_bytes = 2 * rows * columns
    cost = lambda flops, moved: pl.CostEstimate(flops=flops, bytes_accessed=moved, transcendentals=0)

    diagonals = pl.pallas_call(
        gram_kernel,
        out_shape=diag_shape,
        in_specs=[smem, hbm],
        out_specs=vmem,
        scratch_shapes=[held, holders, sems],
        compiler_params=params,
        cost_estimate=cost(gram_flops, x_bytes),
        name="gram_of_step_0",
    )(seating, gradient)
    diagonals = sum_over_devices(diagonals, everywhere)

    turned, diagonals = pl.pallas_call(
        functools.partial(apply_kernel, True),
        out_shape=(x_shape, diag_shape),
        in_specs=[smem, vmem, hbm],
        out_specs=(hbm, vmem),
        scratch_shapes=[held, fold, dense, holders, sems, sems],
        compiler_params=params,
        cost_estimate=cost(gram_flops + turn_flops, 2 * x_bytes),
        name="rotate_step_0",
    )(seating, diagonals, gradient)
    diagonals = sum_over_devices(diagonals, everywhere)

    return pl.pallas_call(
        functools.partial(apply_kernel, False),
        out_shape=x_shape,
        in_specs=[smem, vmem, hbm],
        out_specs=hbm,
        scratch_shapes=[held, fold, dense, holders, sems, sems],
        compiler_params=params,
        cost_estimate=cost(turn_flops, 2 * x_bytes),
        name="rotate_step_1",
    )(following, diagonals, turned)


def solution(mesh):
    in_specs = (P(("wide", "narrow"), None), P())
    out_specs = P(("wide", "narrow"), None)
    return jax.shard_map(
        per_device, mesh=mesh, in_specs=in_specs, out_specs=out_specs, check_vma=False
    )
```

```python
import functools

import jax
import jax.numpy as jnp
from jax import lax
from jax.experimental import pallas as pl
from jax.experimental.pallas import tpu as pltpu
from jax.sharding import PartitionSpec as P

ROUNDS = 8
LANES = 128
VMEM_LIMIT = 56 * 1024 * 1024


def advance(seat_of, total_slots):
    pair_count = total_slots // 2
    cycle_pos = jnp.where(seat_of % 2 == 0, seat_of // 2 - 1, total_slots - 2 - (seat_of - 1) // 2)
    next_pos = (cycle_pos + 1) % (total_slots - 1)
    new_slot = jnp.where(
        next_pos < pair_count - 1, 2 * (next_pos + 1), 2 * (total_slots - 2 - next_pos) + 1
    )
    return jnp.where(seat_of == 0, 0, new_slot)


def cyclic_masks(width):
    row = lax.broadcasted_iota(jnp.int32, (width, width), 0)
    col = lax.broadcasted_iota(jnp.int32, (width, width), 1)
    gap = col - row
    above = jnp.where(gap < 0, gap + width, gap) < ROUNDS
    below = jnp.where(gap > 0, width - gap, -gap) < ROUNDS
    return above, below


def fold(block, mask):
    width = block.shape[0]
    kept = jnp.where(mask, block, 0.0)
    return jnp.sum(kept.reshape(width // ROUNDS, ROUNDS, width), axis=0)


def unfolded(folded, mask):
    width = folded.shape[1]
    tiled = jnp.broadcast_to(folded[None], (width // ROUNDS, ROUNDS, width))
    return jnp.where(mask, tiled.reshape(width, width), 0.0)


def gram_diagonals(left, right):
    width = left.shape[1]
    above, below = cyclic_masks(width)
    over_rows = (((0,), (0,)), ((), ()))
    dot = functools.partial(
        lax.dot_general, dimension_numbers=over_rows, preferred_element_type=jnp.float32
    )
    wide = dot(left, jnp.concatenate([left, right], axis=1))
    cross = wide[:, width:]
    return jnp.concatenate(
        [
            fold(wide[:, :width], above),
            fold(cross, below),
            fold(cross, above),
            fold(dot(right, right), above),
        ],
        axis=0,
    )


def pick(planes, index):
    out = planes[0]
    for place in range(1, len(planes)):
        out = jnp.where(index == place, planes[place], out)
    return out


def roll_lanes(plane, shift):
    width = plane.shape[1]
    shift = shift % width
    return plane if shift == 0 else pltpu.roll(plane, shift, 1)


def blend(c, u, s, v, sign):
    if u is None and v is None:
        return None
    if u is None:
        return s * v if sign > 0 else -(s * v)
    if v is None:
        return c * u
    return c * u + s * v if sign > 0 else c * u - s * v


def rotation_diagonals(load):
    lane = lax.broadcasted_iota(jnp.int32, load(0, 0).shape, 1)
    residue = lane % ROUNDS
    quarters = []
    for q in range(4):
        rows = [load(q, s) for s in range(ROUNDS)]
        if q == 1:
            planes = [pick(rows, (residue + d) % ROUNDS) for d in range(ROUNDS)]
            planes = [roll_lanes(plane, d) for d, plane in enumerate(planes)]
        else:
            planes = [pick(rows, (residue - d) % ROUNDS) for d in range(ROUNDS)]
        quarters.append(planes)
    ll, lr, rl, rr = quarters
    ones = jnp.ones_like(ll[0])
    tl, bl = [ones] + [None] * 7, [None] * 8
    tr, br = [None] * 8, [ones] + [None] * 7
    for r in range(ROUNDS):
        a, c, off = ll[0], rr[0], rl[0]
        spread = c - a
        damping = (a + c) / 16.0 + 1e-06
        rest = 4.0 * off * off + damping * damping
        radius = jnp.sqrt(spread * spread + rest)
        falling = spread < 0.0
        reach = radius + jnp.abs(spread)
        tangent = 2.0 * off * jnp.where(falling, reach, 1.0) / jnp.where(falling, rest, reach)
        cs = 1.0 / jnp.sqrt(1.0 + tangent * tangent)
        sn = tangent * cs
        for rows_l, rows_r in ((tl, tr), (bl, br)):
            for o in range(ROUNDS):
                u, v = rows_l[o], rows_r[o]
                rows_l[o] = blend(cs, u, sn, v, -1)
                rows_r[o] = blend(cs, v, sn, u, 1)
        if r + 1 == ROUNDS:
            break
        needed = ROUNDS - r
        new = [[], [], [], []]
        for d in range(needed):
            cl, sl = roll_lanes(cs, d), roll_lanes(sn, d)
            ll1 = cl * ll[d] - sl * lr[d]
            lr1 = sl * ll[d] + cl * lr[d]
            rl1 = cl * rl[d] - sl * rr[d]
            rr1 = sl * rl[d] + cl * rr[d]
            new[0].append(cs * ll1 - sn * rl1)
            new[1].append(cs * lr1 - sn * rr1)
            new[2].append(sn * ll1 + cs * rl1)
            new[3].append(sn * lr1 + cs * rr1)
        ll = new[0][: needed - 1]
        rl = [roll_lanes(plane, -1) for plane in new[2][1:needed]]
        lr = [rl[0]] + new[1][: needed - 2]
        rr = [roll_lanes(plane, -1) for plane in new[3][: needed - 1]]
        for rows_r in (tr, br):
            rows_r[:] = [None] + [
                None if plane is None else roll_lanes(plane, -1) for plane in rows_r[:-1]
            ]
    folded = []
    for rows in (tl, bl):
        folded.append([pick(rows, (s - residue) % ROUNDS) for s in range(ROUNDS)])
    for rows in (tr, br):
        turned = [roll_lanes(plane, ROUNDS - 1) for plane in rows[::-1]]
        folded.append([pick(turned, (residue - s) % ROUNDS) for s in range(ROUNDS)])
    return folded


def find_holders(seat_ref, holder_ref):
    for block in range(holder_ref.shape[0]):
        holder_ref[seat_ref[block]] = block


def block_copies(pair, holder_ref, outer_ref, pair_buffer, sems, inward):
    width = pair_buffer.shape[2] // 2
    copies = []
    for half in range(2):
        column = pl.multiple_of(holder_ref[2 * pair + half] * width, width)
        outer = outer_ref.at[:, pl.ds(column, width)]
        inner = pair_buffer.at[pair, :, pl.ds(half * width, width)]
        source, target = (outer, inner) if inward else (inner, outer)
        copies.append(pltpu.make_async_copy(source, target, sems.at[2 * pair + half]))
    return copies


def start_all(pairs, make):
    def body(pair, carry):
        for copy in make(pair):
            copy.start()
        return carry

    lax.fori_loop(0, pairs, body, 0)


def wait_all(pairs, make):
    def body(pair, carry):
        for copy in make(pair):
            copy.wait()
        return carry

    lax.fori_loop(0, pairs, body, 0)


def put_pair(ref, pair, value):
    rows = pl.ds(pl.multiple_of(pair * 4 * ROUNDS, 4 * ROUNDS), 4 * ROUNDS)
    for part in range(ref.shape[0]):
        ref[part, rows, :] = value[:, part * LANES : (part + 1) * LANES]


def get_quarter(ref, pair, q):
    rows = pl.ds(pl.multiple_of((pair * 4 + q) * ROUNDS, ROUNDS), ROUNDS)
    return jnp.concatenate([ref[part, rows, :] for part in range(ref.shape[0])], axis=1)


def gram_kernel(seat_ref, x_ref, diag_ref, held, holder_ref, in_sems):
    pairs, _, both = held.shape
    width = both // 2
    find_holders(seat_ref, holder_ref)
    arrive = lambda pair: block_copies(pair, holder_ref, x_ref, held, in_sems, True)
    start_all(pairs, arrive)

    def body(pair, carry):
        for copy in arrive(pair):
            copy.wait()
        put_pair(diag_ref, pair, gram_diagonals(held[pair, :, :width], held[pair, :, width:]))
        return carry

    lax.fori_loop(0, pairs, body, 0)


def store_rotation(diag_ref, fold_ref):
    parts, rows, _ = diag_ref.shape
    pairs = rows // (4 * ROUNDS)
    plane = lambda q, s: pl.ds(q * ROUNDS + s, pairs, stride=4 * ROUNDS)
    load = lambda q, s: jnp.concatenate(
        [diag_ref[part, plane(q, s), :] for part in range(parts)], axis=1
    )
    folded = rotation_diagonals(load)
    for q in range(4):
        for s in range(ROUNDS):
            for part in range(parts):
                columns = slice(part * LANES, (part + 1) * LANES)
                fold_ref[part, plane(q, s), :] = folded[q][s][:, columns]


def rotate_pair(pair, held, fold_ref, dense_ref):
    width = held.shape[2] // 2
    above, below = cyclic_masks(width)
    quarter = lambda q: get_quarter(fold_ref, pair, q)
    dense_ref[:width, :width] = unfolded(quarter(0), below).astype(jnp.bfloat16)
    dense_ref[width:, :width] = unfolded(quarter(1), below).astype(jnp.bfloat16)
    dense_ref[:width, width:] = unfolded(quarter(2), above).astype(jnp.bfloat16)
    dense_ref[width:, width:] = unfolded(quarter(3), above).astype(jnp.bfloat16)
    return jnp.dot(held[pair], dense_ref[...], preferred_element_type=jnp.float32)


def apply_kernel(with_gram, seat_ref, diag_ref, x_ref, *refs):
    if with_gram:
        out_ref, next_ref, held, fold_ref, dense_ref, holder_ref, in_sems, out_sems = refs
    else:
        out_ref, held, fold_ref, dense_ref, holder_ref, in_sems, out_sems = refs
    pairs, _, both = held.shape
    width = both // 2
    find_holders(seat_ref, holder_ref)
    arrive = lambda pair: block_copies(pair, holder_ref, x_ref, held, in_sems, True)
    leave = lambda pair: block_copies(pair, holder_ref, out_ref, held, out_sems, False)
    start_all(pairs, arrive)
    store_rotation(diag_ref, fold_ref)

    def next_gram(pair):
        left_seat = jnp.where(pair == 0, 0, jnp.where(pair == 1, 1, 2 * pair - 2))
        right_seat = jnp.where(pair == pairs - 1, 2 * pairs - 2, 2 * pair + 3)

        def block(seat):
            column = pl.multiple_of((seat % 2) * width, width)
            return held[seat // 2, :, pl.ds(column, width)]

        put_pair(next_ref, pair, gram_diagonals(block(left_seat), block(right_seat)))

    def body(step, carry):
        duo = (2 * step, 2 * step + 1)
        for pair in duo:
            for copy in arrive(pair):
                copy.wait()
        turned = [
            rotate_pair(pair, held, fold_ref, dense_ref.at[slot]) for slot, pair in enumerate(duo)
        ]
        for pair, value in zip(duo, turned):
            held[pair] = value.astype(jnp.bfloat16)
        for pair in duo:
            for copy in leave(pair):
                copy.start()
        if with_gram:
            pl.when(step > 0)(lambda: next_gram(duo[0] - 1))
            next_gram(duo[0])
        return carry

    lax.fori_loop(0, pairs // 2, body, 0)
    if with_gram:
        next_gram(pairs - 1)
    wait_all(pairs, leave)


def sum_over_devices(values, axes, hand_back):
    wide, narrow = (lax.axis_size(axis) for axis in axes)
    count = wide * narrow
    index = lax.axis_index(axes)
    core = narrow
    chips = [[i for i in range(count) if i & core == kind] for kind in (0, core)]

    def swap(x, flip):
        return lax.ppermute(x, axes, [(i, i ^ flip) for i in range(count)])

    def among_chips(x):
        return lax.all_to_all(
            x, axes, split_axis=0, concat_axis=0, axis_index_groups=chips, tiled=True
        )

    held = values.reshape(values.shape[0] * values.shape[1], LANES)
    half = held.shape[0] // 2
    odd = (index & core) != 0
    mine = jnp.where(odd, half, 0)
    keep = lax.dynamic_slice_in_dim(held, mine, half, 0)
    send = lax.dynamic_slice_in_dim(held, half - mine, half, 0)
    held = keep + swap(send, core)
    size = half // (count // 2)
    held = jnp.sum(among_chips(held).reshape(count // 2, size, LANES), axis=0)
    if hand_back == "all_to_all":
        copies = jnp.broadcast_to(held[None], (count // 2, size, LANES))
        held = among_chips(copies.reshape(half, LANES))
    else:
        bits = [1 << b for b in range(count.bit_length() - 1) if 1 << b != core]
        for at in range(0, len(bits), 2):
            pair = bits[at : at + 2]
            group = 1 << len(pair)
            flips = [sum(b for p, b in enumerate(pair) if other >> p & 1) for other in range(group)]
            parts = [held] + [swap(held, flip) for flip in flips[1:]]
            for place, bit in enumerate(pair):
                step = 1 << place
                parts = [
                    jnp.where((index & bit) != 0, parts[at ^ step], parts[at])
                    for at in range(group)
                ]
            held = jnp.concatenate(parts, axis=0)
    other = swap(held, core)
    halves = [jnp.where(odd, other, held), jnp.where(odd, held, other)]
    return jnp.concatenate(halves, axis=0).reshape(values.shape)


def per_device(gradient, seating):
    rows, columns = gradient.shape
    pairs = lax.axis_size("wide")
    width = columns // (2 * pairs)
    everywhere = ("wide", "narrow")
    following = advance(seating, 2 * pairs)

    smem = pl.BlockSpec(memory_space=pltpu.SMEM)
    vmem = pl.BlockSpec(memory_space=pltpu.VMEM)
    hbm = pl.BlockSpec(memory_space=pl.ANY)
    params = pltpu.CompilerParams(vmem_limit_bytes=VMEM_LIMIT)
    held = pltpu.VMEM((pairs, rows, 2 * width), jnp.bfloat16)
    holders = pltpu.SMEM((2 * pairs,), jnp.int32)
    sems = pltpu.SemaphoreType.DMA((2 * pairs,))
    fold = pltpu.VMEM((width // LANES, pairs * 4 * ROUNDS, LANES), jnp.float32)
    dense = pltpu.VMEM((2, 2 * width, 2 * width), jnp.bfloat16)
    diag_shape = jax.ShapeDtypeStruct((width // LANES, pairs * 4 * ROUNDS, LANES), jnp.float32)
    x_shape = jax.ShapeDtypeStruct((rows, columns), jnp.bfloat16)
    gram_flops = 2 * rows * 3 * width * width * pairs
    turn_flops = 2 * rows * 4 * width * width * pairs
    x_bytes = 2 * rows * columns
    cost = lambda flops, moved: pl.CostEstimate(flops=flops, bytes_accessed=moved, transcendentals=0)

    diagonals = pl.pallas_call(
        gram_kernel,
        out_shape=diag_shape,
        in_specs=[smem, hbm],
        out_specs=vmem,
        scratch_shapes=[held, holders, sems],
        compiler_params=params,
        cost_estimate=cost(gram_flops, x_bytes),
        name="gram_of_step_0",
    )(seating, gradient)
    diagonals = sum_over_devices(diagonals, everywhere, "all_to_all")

    turned, diagonals = pl.pallas_call(
        functools.partial(apply_kernel, True),
        out_shape=(x_shape, diag_shape),
        in_specs=[smem, vmem, hbm],
        out_specs=(hbm, vmem),
        scratch_shapes=[held, fold, dense, holders, sems, sems],
        compiler_params=params,
        cost_estimate=cost(gram_flops + turn_flops, 2 * x_bytes),
        name="rotate_step_0",
    )(seating, diagonals, gradient)
    diagonals = sum_over_devices(diagonals, everywhere, "permutes")

    return pl.pallas_call(
        functools.partial(apply_kernel, False),
        out_shape=x_shape,
        in_specs=[smem, vmem, hbm],
        out_specs=hbm,
        scratch_shapes=[held, fold, dense, holders, sems, sems],
        compiler_params=params,
        cost_estimate=cost(turn_flops, 2 * x_bytes),
        name="rotate_step_1",
    )(following, diagonals, turned)


def solution(mesh):
    in_specs = (P(("wide", "narrow"), None), P())
    out_specs = P(("wide", "narrow"), None)
    return jax.shard_map(
        per_device, mesh=mesh, in_specs=in_specs, out_specs=out_specs, check_vma=False
    )
```

```python
import functools

import jax
import jax.numpy as jnp
from jax import lax
from jax.experimental import pallas as pl
from jax.experimental.pallas import tpu as pltpu
from jax.sharding import PartitionSpec as P

ROUNDS = 8
LANES = 128
STRIP = 16
AHEAD = 4
VMEM_LIMIT = 44 * 1024 * 1024


def advance(seat_of, total_slots):
    pair_count = total_slots // 2
    cycle_pos = jnp.where(seat_of % 2 == 0, seat_of // 2 - 1, total_slots - 2 - (seat_of - 1) // 2)
    next_pos = (cycle_pos + 1) % (total_slots - 1)
    new_slot = jnp.where(
        next_pos < pair_count - 1, 2 * (next_pos + 1), 2 * (total_slots - 2 - next_pos) + 1
    )
    return jnp.where(seat_of == 0, 0, new_slot)


def cyclic_masks(width):
    row = lax.broadcasted_iota(jnp.int32, (width, width), 0)
    col = lax.broadcasted_iota(jnp.int32, (width, width), 1)
    gap = col - row
    above = jnp.where(gap < 0, gap + width, gap) < ROUNDS
    below = jnp.where(gap > 0, width - gap, -gap) < ROUNDS
    return above, below


def fold(block, mask):
    width = block.shape[0]
    kept = jnp.where(mask, block, 0.0)
    return jnp.sum(kept.reshape(width // ROUNDS, ROUNDS, width), axis=0)


def unfolded(folded, mask):
    width = folded.shape[1]
    tiled = jnp.broadcast_to(folded[None], (width // ROUNDS, ROUNDS, width))
    return jnp.where(mask, tiled.reshape(width, width), 0.0)


def gram_diagonals(left, right):
    width = left.shape[1]
    above, below = cyclic_masks(width)
    over_rows = (((0,), (0,)), ((), ()))
    dot = functools.partial(
        lax.dot_general, dimension_numbers=over_rows, preferred_element_type=jnp.float32
    )
    wide = dot(left, jnp.concatenate([left, right], axis=1))
    cross = wide[:, width:]
    return jnp.concatenate(
        [
            fold(wide[:, :width], above),
            fold(cross, below),
            fold(cross, above),
            fold(dot(right, right), above),
        ],
        axis=0,
    )


def pick(planes, index):
    out = planes[0]
    for place in range(1, len(planes)):
        out = jnp.where(index == place, planes[place], out)
    return out


def roll_lanes(plane, shift):
    width = plane.shape[1]
    shift = shift % width
    return plane if shift == 0 else pltpu.roll(plane, shift, 1)


def blend(c, u, s, v, sign):
    if u is None and v is None:
        return None
    if u is None:
        return s * v if sign > 0 else -(s * v)
    if v is None:
        return c * u
    return c * u + s * v if sign > 0 else c * u - s * v


def rotation_diagonals(load):
    lane = lax.broadcasted_iota(jnp.int32, load(0, 0).shape, 1)
    residue = lane % ROUNDS
    quarters = []
    for q in range(4):
        rows = [load(q, s) for s in range(ROUNDS)]
        if q == 1:
            planes = [pick(rows, (residue + d) % ROUNDS) for d in range(ROUNDS)]
            planes = [roll_lanes(plane, d) for d, plane in enumerate(planes)]
        else:
            planes = [pick(rows, (residue - d) % ROUNDS) for d in range(ROUNDS)]
        quarters.append(planes)
    ll, lr, rl, rr = quarters
    ones = jnp.ones_like(ll[0])
    tl, bl = [ones] + [None] * 7, [None] * 8
    tr, br = [None] * 8, [ones] + [None] * 7
    for r in range(ROUNDS):
        a, c, off = ll[0], rr[0], rl[0]
        spread = c - a
        damping = (a + c) / 16.0 + 1e-06
        rest = 4.0 * off * off + damping * damping
        radius = jnp.sqrt(spread * spread + rest)
        falling = spread < 0.0
        reach = radius + jnp.abs(spread)
        tangent = 2.0 * off * jnp.where(falling, reach, 1.0) / jnp.where(falling, rest, reach)
        cs = 1.0 / jnp.sqrt(1.0 + tangent * tangent)
        sn = tangent * cs
        for rows_l, rows_r in ((tl, tr), (bl, br)):
            for o in range(ROUNDS):
                u, v = rows_l[o], rows_r[o]
                rows_l[o] = blend(cs, u, sn, v, -1)
                rows_r[o] = blend(cs, v, sn, u, 1)
        if r + 1 == ROUNDS:
            break
        needed = ROUNDS - r
        new = [[], [], [], []]
        for d in range(needed):
            cl, sl = roll_lanes(cs, d), roll_lanes(sn, d)
            ll1 = cl * ll[d] - sl * lr[d]
            lr1 = sl * ll[d] + cl * lr[d]
            rl1 = cl * rl[d] - sl * rr[d]
            rr1 = sl * rl[d] + cl * rr[d]
            new[0].append(cs * ll1 - sn * rl1)
            new[1].append(cs * lr1 - sn * rr1)
            new[2].append(sn * ll1 + cs * rl1)
            new[3].append(sn * lr1 + cs * rr1)
        ll = new[0][: needed - 1]
        rl = [roll_lanes(plane, -1) for plane in new[2][1:needed]]
        lr = [rl[0]] + new[1][: needed - 2]
        rr = [roll_lanes(plane, -1) for plane in new[3][: needed - 1]]
        for rows_r in (tr, br):
            rows_r[:] = [None] + [
                None if plane is None else roll_lanes(plane, -1) for plane in rows_r[:-1]
            ]
    folded = []
    for rows in (tl, bl):
        folded.append([pick(rows, (s - residue) % ROUNDS) for s in range(ROUNDS)])
    for rows in (tr, br):
        turned = [roll_lanes(plane, ROUNDS - 1) for plane in rows[::-1]]
        folded.append([pick(turned, (residue - s) % ROUNDS) for s in range(ROUNDS)])
    return folded


def find_holders(seat_ref, holder_ref):
    for block in range(holder_ref.shape[0]):
        holder_ref[seat_ref[block]] = block


def block_copies(pair, holder_ref, outer_ref, pair_buffer, sems, inward):
    width = pair_buffer.shape[2] // 2
    copies = []
    for half in range(2):
        column = pl.multiple_of(holder_ref[2 * pair + half] * width, width)
        outer = outer_ref.at[:, pl.ds(column, width)]
        inner = pair_buffer.at[pair, :, pl.ds(half * width, width)]
        source, target = (outer, inner) if inward else (inner, outer)
        copies.append(pltpu.make_async_copy(source, target, sems.at[2 * pair + half]))
    return copies


def start_each(pairs, make):
    def body(pair, carry):
        for copy in make(pair):
            copy.start()
        return carry

    lax.fori_loop(0, pairs, body, 0)


def wait_all(pairs, make):
    def body(pair, carry):
        for copy in make(pair):
            copy.wait()
        return carry

    lax.fori_loop(0, pairs, body, 0)


def second_core():
    return lax.axis_index("wide") % 2 == 1


def put_pair(keep_ref, send_ref, pair, value):
    rows = pl.ds(pl.multiple_of(pair * 4 * ROUNDS, 4 * ROUNDS), 4 * ROUNDS)
    first, second = value[:, :LANES], value[:, LANES:]
    odd = second_core()
    keep_ref[rows, :] = jnp.where(odd, second, first)
    send_ref[rows, :] = jnp.where(odd, first, second)


def get_quarter(ref, pair, q):
    rows = pl.ds(pl.multiple_of((pair * 4 + q) * ROUNDS, ROUNDS), ROUNDS)
    return jnp.concatenate([ref[part, rows, :] for part in range(ref.shape[0])], axis=1)


def gram_kernel(seat_ref, x_ref, keep_ref, send_ref, held, holder_ref, in_sems):
    pairs, _, both = held.shape
    width = both // 2
    find_holders(seat_ref, holder_ref)
    arrive = lambda pair: block_copies(pair, holder_ref, x_ref, held, in_sems, True)
    start_each(AHEAD, arrive)

    def body(pair, carry):
        @pl.when(pair + AHEAD < pairs)
        def _():
            for copy in arrive(pair + AHEAD):
                copy.start()

        for copy in arrive(pair):
            copy.wait()
        put_pair(keep_ref, send_ref, pair, gram_diagonals(held[pair, :, :width], held[pair, :, width:]))
        return carry

    lax.fori_loop(0, pairs, body, 0)


def store_rotation(own_ref, other_ref, fold_ref):
    parts, rows, _ = fold_ref.shape
    pairs = rows // (4 * ROUNDS)
    plane = lambda q, s: pl.ds(q * ROUNDS + s, pairs, stride=4 * ROUNDS)
    odd = second_core()

    def load(q, s):
        own, other = own_ref[plane(q, s), :], other_ref[plane(q, s), :]
        halves = [jnp.where(odd, other, own), jnp.where(odd, own, other)]
        return jnp.concatenate(halves, axis=1)

    folded = rotation_diagonals(load)
    for q in range(4):
        for s in range(ROUNDS):
            for part in range(parts):
                columns = slice(part * LANES, (part + 1) * LANES)
                fold_ref[part, plane(q, s), :] = folded[q][s][:, columns]


def rotate_pair(pair, held, fold_ref, dense_ref):
    width = held.shape[2] // 2
    above, below = cyclic_masks(width)
    quarter = lambda q: get_quarter(fold_ref, pair, q)
    for column in range(2):
        for row in range(2):
            spread = unfolded(quarter(2 * column + row), above if column else below)
            spread = spread.astype(jnp.bfloat16)
            for part in range(0, width, LANES):
                for other in range(0, width, LANES):
                    if part == other:
                        rows = slice(part, part + LANES)
                    elif column:
                        rows = slice(part + LANES - STRIP, part + LANES)
                    else:
                        rows = slice(part, part + STRIP)
                    columns = slice(column * width + other, column * width + other + LANES)
                    shifted = slice(row * width + rows.start, row * width + rows.stop)
                    dense_ref[shifted, columns] = spread[rows, other : other + LANES]
    return jnp.dot(held[pair], dense_ref[...], preferred_element_type=jnp.float32)


def apply_kernel(with_gram, seat_ref, own_ref, other_ref, x_ref, *refs):
    if with_gram:
        out_ref, keep_ref, send_ref, held, fold_ref, dense_ref, holder_ref, in_sems, out_sems = refs
    else:
        out_ref, held, fold_ref, dense_ref, holder_ref, in_sems, out_sems = refs
    pairs, _, both = held.shape
    width = both // 2
    find_holders(seat_ref, holder_ref)
    arrive = lambda pair: block_copies(pair, holder_ref, x_ref, held, in_sems, True)
    leave = lambda pair: block_copies(pair, holder_ref, out_ref, held, out_sems, False)
    start_each(AHEAD, arrive)
    dense_ref[...] = jnp.zeros_like(dense_ref)
    store_rotation(own_ref, other_ref, fold_ref)

    def next_gram(pair):
        left_seat = jnp.where(pair == 0, 0, jnp.where(pair == 1, 1, 2 * pair - 2))
        right_seat = jnp.where(pair == pairs - 1, 2 * pairs - 2, 2 * pair + 3)

        def block(seat):
            column = pl.multiple_of((seat % 2) * width, width)
            return held[seat // 2, :, pl.ds(column, width)]

        put_pair(keep_ref, send_ref, pair, gram_diagonals(block(left_seat), block(right_seat)))

    def body(step, carry):
        duo = (2 * step, 2 * step + 1)

        @pl.when(2 * step + AHEAD < pairs)
        def _():
            for pair in duo:
                for copy in arrive(pair + AHEAD):
                    copy.start()

        for pair in duo:
            for copy in arrive(pair):
                copy.wait()
        turned = [
            rotate_pair(pair, held, fold_ref, dense_ref.at[slot]) for slot, pair in enumerate(duo)
        ]
        for pair, value in zip(duo, turned):
            held[pair] = value.astype(jnp.bfloat16)
        for pair in duo:
            for copy in leave(pair):
                copy.start()
        if with_gram:
            pl.when(step > 0)(lambda: next_gram(duo[0] - 1))
            next_gram(duo[0])
        return carry

    lax.fori_loop(0, pairs // 2, body, 0)
    if with_gram:
        next_gram(pairs - 1)
    wait_all(pairs, leave)


def sum_over_devices(keep, send, axes):
    wide, narrow = (lax.axis_size(axis) for axis in axes)
    count = wide * narrow
    core, group = narrow, count // 2
    chips = [[i for i in range(count) if i & core == kind] for kind in (0, core)]
    partner = [(i, i ^ core) for i in range(count)]

    def among_chips(x):
        return lax.all_to_all(
            x, axes, split_axis=0, concat_axis=0, axis_index_groups=chips, tiled=True
        )

    rows = keep.shape[0]
    held = among_chips(keep + lax.ppermute(send, axes, partner))
    held = jnp.sum(held.reshape(group, rows // group, LANES), axis=0)
    copies = jnp.broadcast_to(held[None], (group, rows // group, LANES))
    own = among_chips(copies.reshape(rows, LANES))
    return own, lax.ppermute(own, axes, partner)


def per_device(gradient, seating):
    rows, columns = gradient.shape
    pairs = lax.axis_size("wide")
    width = columns // (2 * pairs)
    assert width == 2 * LANES and pairs >= AHEAD
    everywhere = ("wide", "narrow")
    following = advance(seating, 2 * pairs)

    smem = pl.BlockSpec(memory_space=pltpu.SMEM)
    vmem = pl.BlockSpec(memory_space=pltpu.VMEM)
    hbm = pl.BlockSpec(memory_space=pl.ANY)
    params = pltpu.CompilerParams(vmem_limit_bytes=VMEM_LIMIT)
    held = pltpu.VMEM((pairs, rows, 2 * width), jnp.bfloat16)
    holders = pltpu.SMEM((2 * pairs,), jnp.int32)
    sems = pltpu.SemaphoreType.DMA((2 * pairs,))
    fold = pltpu.VMEM((width // LANES, pairs * 4 * ROUNDS, LANES), jnp.float32)
    dense = pltpu.VMEM((2, 2 * width, 2 * width), jnp.bfloat16)
    diag_shape = jax.ShapeDtypeStruct((pairs * 4 * ROUNDS, LANES), jnp.float32)
    x_shape = jax.ShapeDtypeStruct((rows, columns), jnp.bfloat16)
    gram_flops = 2 * rows * 3 * width * width * pairs
    turn_flops = 2 * rows * 4 * width * width * pairs
    x_bytes = 2 * rows * columns
    cost = lambda flops, moved: pl.CostEstimate(flops=flops, bytes_accessed=moved, transcendentals=0)

    keep, send = pl.pallas_call(
        gram_kernel,
        out_shape=(diag_shape, diag_shape),
        in_specs=[smem, hbm],
        out_specs=(vmem, vmem),
        scratch_shapes=[held, holders, sems],
        compiler_params=params,
        cost_estimate=cost(gram_flops, x_bytes),
        name="gram_of_step_0",
    )(seating, gradient)
    own, other = sum_over_devices(keep, send, everywhere)

    turned, keep, send = pl.pallas_call(
        functools.partial(apply_kernel, True),
        out_shape=(x_shape, diag_shape, diag_shape),
        in_specs=[smem, vmem, vmem, hbm],
        out_specs=(hbm, vmem, vmem),
        scratch_shapes=[held, fold, dense, holders, sems, sems],
        compiler_params=params,
        cost_estimate=cost(gram_flops + turn_flops, 2 * x_bytes),
        name="rotate_step_0",
    )(seating, own, other, gradient)
    own, other = sum_over_devices(keep, send, everywhere)

    return pl.pallas_call(
        functools.partial(apply_kernel, False),
        out_shape=x_shape,
        in_specs=[smem, vmem, vmem, hbm],
        out_specs=hbm,
        scratch_shapes=[held, fold, dense, holders, sems, sems],
        compiler_params=params,
        cost_estimate=cost(turn_flops, 2 * x_bytes),
        name="rotate_step_1",
    )(following, own, other, turned)


def solution(mesh):
    in_specs = (P(("wide", "narrow"), None), P())
    out_specs = P(("wide", "narrow"), None)
    return jax.shard_map(
        per_device, mesh=mesh, in_specs=in_specs, out_specs=out_specs, check_vma=False
    )
```

```python
import functools

import jax
import jax.numpy as jnp
from jax import lax
from jax.experimental import pallas as pl
from jax.experimental.pallas import tpu as pltpu
from jax.sharding import PartitionSpec as P

ROUNDS = 8
LANES = 128
STRIP = 16
AHEAD = 4
VMEM_LIMIT = 44 * 1024 * 1024


def advance(seat_of, total_slots):
    pair_count = total_slots // 2
    cycle_pos = jnp.where(seat_of % 2 == 0, seat_of // 2 - 1, total_slots - 2 - (seat_of - 1) // 2)
    next_pos = (cycle_pos + 1) % (total_slots - 1)
    new_slot = jnp.where(
        next_pos < pair_count - 1, 2 * (next_pos + 1), 2 * (total_slots - 2 - next_pos) + 1
    )
    return jnp.where(seat_of == 0, 0, new_slot)


def window_masks(rows, before):
    row = lax.broadcasted_iota(jnp.int32, (rows, LANES), 0) - before
    col = lax.broadcasted_iota(jnp.int32, (rows, LANES), 1)
    gap = col - row
    return (gap >= 0) & (gap < ROUNDS), (gap <= 0) & (gap > -ROUNDS)


def fold(block, upper):
    width = block.shape[0]
    before = ROUNDS if upper else 0
    window = LANES + ROUNDS
    mask = window_masks(window, before)[0 if upper else 1]
    parts = []
    for part in range(0, width, LANES):
        strip = (part - ROUNDS if upper else part + LANES) % width
        pieces = [
            block[strip : strip + ROUNDS, part : part + LANES],
            block[part : part + LANES, part : part + LANES],
        ]
        kept = jnp.where(mask, jnp.concatenate(pieces if upper else pieces[::-1], axis=0), 0.0)
        parts.append(jnp.sum(kept.reshape(window // ROUNDS, ROUNDS, LANES), axis=0))
    return jnp.concatenate(parts, axis=1)


def gram_diagonals(left, right):
    width = left.shape[1]
    over_rows = (((0,), (0,)), ((), ()))
    dot = functools.partial(
        lax.dot_general, dimension_numbers=over_rows, preferred_element_type=jnp.float32
    )
    wide = dot(left, jnp.concatenate([left, right], axis=1))
    cross = wide[:, width:]
    return jnp.concatenate(
        [
            fold(wide[:, :width], True),
            fold(cross, False),
            fold(cross, True),
            fold(dot(right, right), True),
        ],
        axis=0,
    )


def turn(planes, sign):
    lane = lax.broadcasted_iota(jnp.int32, planes[0].shape, 1)
    step = 1
    while step < ROUNDS:
        moves = (lane & step) != 0
        planes = [
            jnp.where(moves, planes[(j + sign * step) % ROUNDS], planes[j]) for j in range(ROUNDS)
        ]
        step *= 2
    return planes


def roll_lanes(plane, shift):
    width = plane.shape[1]
    shift = shift % width
    return plane if shift == 0 else pltpu.roll(plane, shift, 1)


def blend(c, u, s, v, sign):
    if u is None and v is None:
        return None
    if u is None:
        return s * v if sign > 0 else -(s * v)
    if v is None:
        return c * u
    return c * u + s * v if sign > 0 else c * u - s * v


def rotation_diagonals(load):
    quarters = []
    for q in range(4):
        turned = turn([load(q, s) for s in range(ROUNDS)], 1)
        if q == 1:
            quarters.append([roll_lanes(turned[d], d) for d in range(ROUNDS)])
        else:
            quarters.append([turned[-d] for d in range(ROUNDS)])
    ll, lr, rl, rr = (dict(enumerate(planes)) for planes in quarters)
    for d in range(1, ROUNDS):
        ll[-d], rr[-d] = roll_lanes(ll[d], -d), roll_lanes(rr[d], -d)
        lr[-d], rl[-d] = roll_lanes(rl[d], -d), roll_lanes(lr[d], -d)
    ones = jnp.ones_like(ll[0])
    tl, bl = [ones] + [None] * 7, [None] * 8
    tr, br = [None] * 8, [ones] + [None] * 7
    for r in range(ROUNDS):
        a, c, off = ll[0], rr[0], lr[0]
        spread = c - a
        damping = (a + c) / 16.0 + 1e-06
        radius = jnp.sqrt(spread * spread + 4.0 * off * off + damping * damping)
        tangent = 2.0 * off / (spread + radius)
        cs = 1.0 / jnp.sqrt(1.0 + tangent * tangent)
        sn = tangent * cs
        for rows_l, rows_r in ((tl, tr), (bl, br)):
            for o in range(ROUNDS):
                u, v = rows_l[o], rows_r[o]
                rows_l[o] = blend(cs, u, sn, v, -1)
                rows_r[o] = blend(cs, v, sn, u, 1)
        if r + 1 == ROUNDS:
            break
        reach = ROUNDS - 1 - r
        new = [{}, {}, {}, {}]
        for d in range(-reach, reach + 1):
            cl, sl = roll_lanes(cs, d), roll_lanes(sn, d)
            ll1 = cl * ll[d] - sl * lr[d]
            lr1 = sl * ll[d] + cl * lr[d]
            rl1 = cl * rl[d] - sl * rr[d]
            rr1 = sl * rl[d] + cl * rr[d]
            new[0][d] = cs * ll1 - sn * rl1
            new[1][d] = cs * lr1 - sn * rr1
            new[2][d] = sn * ll1 + cs * rl1
            new[3][d] = sn * lr1 + cs * rr1
        inner = range(1 - reach, reach)
        ll = {d: new[0][d] for d in inner}
        lr = {d: new[1][d - 1] for d in inner}
        rl = {d: roll_lanes(new[2][d + 1], -1) for d in inner}
        rr = {d: roll_lanes(new[3][d], -1) for d in inner}
        for rows_r in (tr, br):
            rows_r[:] = [None] + [
                None if plane is None else roll_lanes(plane, -1) for plane in rows_r[:-1]
            ]
    folded = []
    for rows in (tl, bl):
        folded.append(turn(rows, -1))
    for rows in (tr, br):
        turned = turn([roll_lanes(plane, ROUNDS - 1) for plane in rows[::-1]], 1)
        folded.append([turned[-s] for s in range(ROUNDS)])
    return folded


def find_holders(seat_ref, holder_ref):
    for block in range(holder_ref.shape[0]):
        holder_ref[seat_ref[block]] = block


def block_copies(pair, holder_ref, outer_ref, pair_buffer, sems, inward):
    width = pair_buffer.shape[2] // 2
    copies = []
    for half in range(2):
        column = pl.multiple_of(holder_ref[2 * pair + half] * width, width)
        outer = outer_ref.at[:, pl.ds(column, width)]
        inner = pair_buffer.at[pair, :, pl.ds(half * width, width)]
        source, target = (outer, inner) if inward else (inner, outer)
        copies.append(pltpu.make_async_copy(source, target, sems.at[2 * pair + half]))
    return copies


def start_each(pairs, make):
    def body(pair, carry):
        for copy in make(pair):
            copy.start()
        return carry

    lax.fori_loop(0, pairs, body, 0)


def wait_all(pairs, make):
    def body(pair, carry):
        for copy in make(pair):
            copy.wait()
        return carry

    lax.fori_loop(0, pairs, body, 0)


def second_core():
    return lax.axis_index("wide") % 2 == 1


def put_pair(keep_ref, send_ref, pair, value):
    rows = pl.ds(pl.multiple_of(pair * 4 * ROUNDS, 4 * ROUNDS), 4 * ROUNDS)
    first, second = value[:, :LANES], value[:, LANES:]
    odd = second_core()
    keep_ref[rows, :] = jnp.where(odd, second, first)
    send_ref[rows, :] = jnp.where(odd, first, second)


def get_quarter(ref, pair, q):
    rows = pl.ds(pl.multiple_of((pair * 4 + q) * ROUNDS, ROUNDS), ROUNDS)
    return jnp.concatenate([ref[part, rows, :] for part in range(ref.shape[0])], axis=1)


def gram_kernel(seat_ref, x_ref, keep_ref, send_ref, held, holder_ref, in_sems):
    pairs, _, both = held.shape
    width = both // 2
    find_holders(seat_ref, holder_ref)
    arrive = lambda pair: block_copies(pair, holder_ref, x_ref, held, in_sems, True)
    start_each(AHEAD, arrive)

    def body(pair, carry):
        @pl.when(pair + AHEAD < pairs)
        def _():
            for copy in arrive(pair + AHEAD):
                copy.start()

        for copy in arrive(pair):
            copy.wait()
        put_pair(keep_ref, send_ref, pair, gram_diagonals(held[pair, :, :width], held[pair, :, width:]))
        return carry

    lax.fori_loop(0, pairs, body, 0)


def store_rotation(own_ref, other_ref, fold_ref):
    parts, rows, _ = fold_ref.shape
    pairs = rows // (4 * ROUNDS)
    plane = lambda q, s: pl.ds(q * ROUNDS + s, pairs, stride=4 * ROUNDS)
    odd = second_core()

    def load(q, s):
        own, other = own_ref[plane(q, s), :], other_ref[plane(q, s), :]
        halves = [jnp.where(odd, other, own), jnp.where(odd, own, other)]
        return jnp.concatenate(halves, axis=1)

    folded = rotation_diagonals(load)
    for q in range(4):
        for s in range(ROUNDS):
            for part in range(parts):
                columns = slice(part * LANES, (part + 1) * LANES)
                fold_ref[part, plane(q, s), :] = folded[q][s][:, columns]


def rotate_pair(pair, held, fold_ref, dense_ref):
    width = held.shape[2] // 2
    window = LANES + STRIP
    above = window_masks(window, STRIP)[0]
    below = window_masks(window, 0)[1]
    for column in range(2):
        for row in range(2):
            folded = get_quarter(fold_ref, pair, 2 * column + row)
            for part in range(0, width, LANES):
                tiled = jnp.broadcast_to(
                    folded[None, :, part : part + LANES], (window // ROUNDS, ROUNDS, LANES)
                ).reshape(window, LANES)
                spread = jnp.where(above if column else below, tiled, 0.0).astype(jnp.bfloat16)
                block = spread[STRIP:] if column else spread[:LANES]
                beside = spread[:STRIP] if column else spread[LANES:]
                strip = row * width + (part - STRIP if column else part + LANES) % width
                columns = slice(column * width + part, column * width + part + LANES)
                dense_ref[row * width + part : row * width + part + LANES, columns] = block
                dense_ref[strip : strip + STRIP, columns] = beside
    return jnp.dot(held[pair], dense_ref[...], preferred_element_type=jnp.float32)


def apply_kernel(with_gram, seat_ref, own_ref, other_ref, x_ref, *refs):
    if with_gram:
        out_ref, keep_ref, send_ref, held, fold_ref, dense_ref, holder_ref, in_sems, out_sems = refs
    else:
        out_ref, held, fold_ref, dense_ref, holder_ref, in_sems, out_sems = refs
    pairs, _, both = held.shape
    width = both // 2
    find_holders(seat_ref, holder_ref)
    arrive = lambda pair: block_copies(pair, holder_ref, x_ref, held, in_sems, True)
    leave = lambda pair: block_copies(pair, holder_ref, out_ref, held, out_sems, False)
    start_each(pairs, arrive)
    dense_ref[...] = jnp.zeros_like(dense_ref)
    store_rotation(own_ref, other_ref, fold_ref)

    def next_gram(pair):
        left_seat = jnp.where(pair == 0, 0, jnp.where(pair == 1, 1, 2 * pair - 2))
        right_seat = jnp.where(pair == pairs - 1, 2 * pairs - 2, 2 * pair + 3)

        def block(seat):
            column = pl.multiple_of((seat % 2) * width, width)
            return held[seat // 2, :, pl.ds(column, width)]

        put_pair(keep_ref, send_ref, pair, gram_diagonals(block(left_seat), block(right_seat)))

    def body(step, carry):
        duo = (2 * step, 2 * step + 1)

        for pair in duo:
            for copy in arrive(pair):
                copy.wait()
        turned = [
            rotate_pair(pair, held, fold_ref, dense_ref.at[slot]) for slot, pair in enumerate(duo)
        ]
        for pair, value in zip(duo, turned):
            held[pair] = value.astype(jnp.bfloat16)
        for pair in duo:
            for copy in leave(pair):
                copy.start()
        if with_gram:
            pl.when(step > 0)(lambda: next_gram(duo[0] - 1))
            next_gram(duo[0])
        return carry

    lax.fori_loop(0, pairs // 2, body, 0)
    if with_gram:
        next_gram(pairs - 1)
    wait_all(pairs, leave)


def sum_over_devices(keep, send, axes):
    wide, narrow = (lax.axis_size(axis) for axis in axes)
    count = wide * narrow
    core, group = narrow, count // 2
    chips = [[i for i in range(count) if i & core == kind] for kind in (0, core)]
    partner = [(i, i ^ core) for i in range(count)]

    def among_chips(x):
        return lax.all_to_all(
            x, axes, split_axis=0, concat_axis=0, axis_index_groups=chips, tiled=True
        )

    rows = keep.shape[0]
    held = among_chips(keep + lax.ppermute(send, axes, partner))
    held = jnp.sum(held.reshape(group, rows // group, LANES), axis=0)
    copies = jnp.broadcast_to(held[None], (group, rows // group, LANES))
    own = among_chips(copies.reshape(rows, LANES))
    return own, lax.ppermute(own, axes, partner)


def per_device(gradient, seating):
    rows, columns = gradient.shape
    pairs = lax.axis_size("wide")
    width = columns // (2 * pairs)
    assert width == 2 * LANES and pairs >= AHEAD
    everywhere = ("wide", "narrow")
    following = advance(seating, 2 * pairs)

    smem = pl.BlockSpec(memory_space=pltpu.SMEM)
    vmem = pl.BlockSpec(memory_space=pltpu.VMEM)
    hbm = pl.BlockSpec(memory_space=pl.ANY)
    params = pltpu.CompilerParams(vmem_limit_bytes=VMEM_LIMIT)
    held = pltpu.VMEM((pairs, rows, 2 * width), jnp.bfloat16)
    holders = pltpu.SMEM((2 * pairs,), jnp.int32)
    sems = pltpu.SemaphoreType.DMA((2 * pairs,))
    fold = pltpu.VMEM((width // LANES, pairs * 4 * ROUNDS, LANES), jnp.float32)
    dense = pltpu.VMEM((2, 2 * width, 2 * width), jnp.bfloat16)
    diag_shape = jax.ShapeDtypeStruct((pairs * 4 * ROUNDS, LANES), jnp.float32)
    x_shape = jax.ShapeDtypeStruct((rows, columns), jnp.bfloat16)
    gram_flops = 2 * rows * 3 * width * width * pairs
    turn_flops = 2 * rows * 4 * width * width * pairs
    x_bytes = 2 * rows * columns
    cost = lambda flops, moved: pl.CostEstimate(flops=flops, bytes_accessed=moved, transcendentals=0)

    keep, send = pl.pallas_call(
        gram_kernel,
        out_shape=(diag_shape, diag_shape),
        in_specs=[smem, hbm],
        out_specs=(vmem, vmem),
        scratch_shapes=[held, holders, sems],
        compiler_params=params,
        cost_estimate=cost(gram_flops, x_bytes),
        name="gram_of_step_0",
    )(seating, gradient)
    own, other = sum_over_devices(keep, send, everywhere)

    turned, keep, send = pl.pallas_call(
        functools.partial(apply_kernel, True),
        out_shape=(x_shape, diag_shape, diag_shape),
        in_specs=[smem, vmem, vmem, hbm],
        out_specs=(hbm, vmem, vmem),
        scratch_shapes=[held, fold, dense, holders, sems, sems],
        compiler_params=params,
        cost_estimate=cost(gram_flops + turn_flops, 2 * x_bytes),
        name="rotate_step_0",
    )(seating, own, other, gradient)
    own, other = sum_over_devices(keep, send, everywhere)

    return pl.pallas_call(
        functools.partial(apply_kernel, False),
        out_shape=x_shape,
        in_specs=[smem, vmem, vmem, hbm],
        out_specs=hbm,
        scratch_shapes=[held, fold, dense, holders, sems, sems],
        compiler_params=params,
        cost_estimate=cost(turn_flops, 2 * x_bytes),
        name="rotate_step_1",
    )(following, own, other, turned)


def solution(mesh):
    in_specs = (P(("wide", "narrow"), None), P())
    out_specs = P(("wide", "narrow"), None)
    return jax.shard_map(
        per_device, mesh=mesh, in_specs=in_specs, out_specs=out_specs, check_vma=False
    )
```
